32 devices in a mesh: dp: 8 (over y, x, core), tensor: 4 (over z).
Axes of the slice: x: 2, y: 2, z: 4, core: 2. Of those that a mesh axis runs over, the one named last changes fastest.
Arguments:
- queries: bfloat16 [1024, 16384], P('dp', 'tensor'), may hold values from -24 to 24
- draft_keys: bfloat16 [1024, 1024], P('dp'), may hold values from -6 to 6
- draft_values: bfloat16 [1024, 1024], P('dp'), may hold values from -6 to 6
- cache_keys: bfloat16 [16, 2048, 1024], P('dp', 'tensor'), may hold values from -24 to 24
- cache_values: bfloat16 [16, 2048, 1024], P('dp', 'tensor'), may hold values from -6 to 6
- out_weight: bfloat16 [16384, 16384], P('tensor', 'dp'), may hold values from -0.25 to 0.25
- cache_lengths: int32 [16], P('dp'), may hold values from 512 to 2048
- draft_lengths: int32 [16], replicated, may hold values from 8 to 64
- dest_group: int32 [16], replicated, may hold values from 0 to 7, as said below
- dest_offset: int32 [16], replicated, may hold values from 0 to 32, as said below
Outputs:
- verified: bfloat16 [768, 16384], P('tensor', 'dp')
The draws below stay inside these ranges and needn't reach their ends.
Inputs may be any that keep to these rules, and one draw needn't show every extreme that they name: `dest_group`: at most one request of a group has another group as destination, and each group receives at most one such request. `dest_offset`: blocks with the same destination never intersect and end at packed row 96 or before; a block moved to another group starts right after that group's own rows; in every draw some group's blocks fill all 96 rows.
All inputs are finite; a program needn't handle non-finite values.
Results may differ from the reference program's by a relative error of at most 0.017.
Values may be sent and summed in bfloat16 or wider, within the bound.
A program may use at most 128 MiB of HBM per device.

```python
import jax
import jax.numpy as jnp
from jax import lax

MODEL_DIM = 16384
HEADS = 128
KV_HEADS = 8
HEAD_DIM = 128
DRAFT = 64
GROUP_REQ = 2
CACHE = 2048
PACK = 96
REQUESTS = 16
TOKENS = 1024
ROWS = 768
N_TENSOR = 4


def draw_queries(key, part):
    base_draw = 2.0 * jnp.clip(jax.random.normal(jax.random.fold_in(key, 1), (TOKENS, HEADS * HEAD_DIM), jnp.float32), -6.0, 6.0)
    return jnp.clip(base_draw, -24.0, 24.0).astype(jnp.bfloat16)


def draw_cache_keys(key, part):
    base_draw = jnp.clip(jax.random.normal(jax.random.fold_in(key, 3), (REQUESTS, CACHE, KV_HEADS * HEAD_DIM), jnp.float32), -6.0, 6.0)
    return jnp.clip(base_draw, -24.0, 24.0).astype(jnp.bfloat16)


def plan_tables(key):
    groups = REQUESTS // GROUP_REQ
    half_count = groups // 2
    group_order = jax.random.permutation(jax.random.fold_in(key, 101), groups).astype(jnp.int32)
    group_place = jnp.zeros((groups,), jnp.int32).at[group_order].set(jnp.arange(groups, dtype=jnp.int32))
    is_heavy = group_place < half_count
    partner = group_order[(group_place + half_count) % groups]
    long_len = jax.random.randint(jax.random.fold_in(key, 102), (groups, 2), 3 * DRAFT // 4, DRAFT + 1, jnp.int32)
    short_len = jax.random.randint(jax.random.fold_in(key, 103), (groups, 2), 8, DRAFT // 4 + 1, jnp.int32)
    lengths = jnp.where(is_heavy[:, None], long_len, short_len)
    lengths = lengths.at[group_order[0], 1].set(DRAFT)
    lengths = lengths.at[group_order[half_count]].set(DRAFT // 4)
    own_group = jnp.arange(groups, dtype=jnp.int32)
    dest = jnp.stack([own_group, jnp.where(is_heavy, partner, own_group)], axis=1)
    light_load = lengths[:, 0] + lengths[:, 1]
    offset = jnp.stack([jnp.zeros((groups,), jnp.int32), jnp.where(is_heavy, light_load[partner], lengths[:, 0])], axis=1)
    return (lengths.reshape(-1).astype(jnp.int32), dest.reshape(-1).astype(jnp.int32), offset.reshape(-1).astype(jnp.int32))


def draw_draft_lengths(key, part):
    return plan_tables(key)[0]


def draw_dest_group(key, part):
    return plan_tables(key)[1]


def draw_dest_offset(key, part):
    return plan_tables(key)[2]


def plant(result, own_key, low, largest):
    shape = result.shape
    index_at = [jax.random.randint(jax.random.fold_in(own_key, axis), (), 0, shape[axis]) for axis in range(len(shape))]
    result = result.at[tuple(index_at)].set(low)
    longest = shape.index(max(shape))
    index_at[longest] = (index_at[longest] + 1) % shape[longest]
    return result.at[tuple(index_at)].set(largest)


def levels(own_key, shape, pieces, low, top_value):
    factor_of, own = 1.0, jax.random.fold_in(own_key, 6)
    for axis_at, blocks in pieces:
        steps = jnp.exp(jax.random.uniform(jax.random.fold_in(own, axis_at), (blocks,), jnp.float32, low / len(pieces), top_value / len(pieces)))
        factor_of = factor_of * jnp.repeat(steps, shape[axis_at] // blocks).reshape([-1 if axis == axis_at else 1 for axis in range(len(shape))])
    return factor_of


def bell_draw(stream_key, extent, spread, reach, pieces=(), kind=jnp.bfloat16):
    entries = spread * jax.random.normal(stream_key, extent, jnp.float32)
    if pieces:
        entries = entries * levels(stream_key, extent, pieces, -0.22, 0.18)
    return jnp.clip(entries, -reach, reach).astype(kind)


def setup_inputs(seed: int = 0) -> dict:
    arg_keys = jax.random.split(jax.random.key(seed), 11)
    return {
        "queries": draw_queries(jax.random.fold_in(arg_keys[10], 71), 0),
        "draft_keys": bell_draw(arg_keys[1], (TOKENS, KV_HEADS * HEAD_DIM), 1.0, 6.0, ((0, 8),)),
        "draft_values": bell_draw(arg_keys[2], (TOKENS, KV_HEADS * HEAD_DIM), 1.0, 6.0, ((0, 8),)),
        "cache_keys": draw_cache_keys(jax.random.fold_in(arg_keys[10], 71), 0),
        "cache_values": bell_draw(arg_keys[4], (REQUESTS, CACHE, KV_HEADS * HEAD_DIM), 1.0, 6.0, ((0, 8), (1, 4))),
        "out_weight": bell_draw(arg_keys[5], (HEADS * HEAD_DIM, MODEL_DIM), (HEADS * HEAD_DIM // 32) ** -0.5, 0.25, ((0, 4), (1, 8))),
        "cache_lengths": plant(jax.random.randint(arg_keys[6], (REQUESTS,), CACHE // 4, CACHE + 1), jax.random.fold_in(arg_keys[6], 1), CACHE // 4, CACHE).astype(jnp.int32),
        "draft_lengths": draw_draft_lengths(jax.random.fold_in(arg_keys[10], 71), 0),
        "dest_group": draw_dest_group(jax.random.fold_in(arg_keys[10], 71), 0),
        "dest_offset": draw_dest_offset(jax.random.fold_in(arg_keys[10], 71), 0),
    }


NEG_FILL = -1e30


def packed_sources(row_ids, draft_lengths, dest_group, dest_offset):
    request_ids = jnp.arange(dest_group.shape[0], dtype=jnp.int32)
    slot_group = row_ids // PACK
    slot_index = row_ids % PACK
    inside = (dest_group[None, :] == slot_group[:, None]) & (slot_index[:, None] >= dest_offset[None, :]) & (slot_index[:, None] < (dest_offset + draft_lengths)[None, :])
    request = jnp.sum(jnp.where(inside, request_ids[None, :], 0), axis=1).astype(jnp.int32)
    first_slot = jnp.sum(jnp.where(inside, dest_offset[None, :], 0), axis=1).astype(jnp.int32)
    return request, (slot_index - first_slot).astype(jnp.int32), jnp.any(inside, axis=1)


def attend_request(operands):
    queries_one, cache_k, cache_v, draft_k, draft_v, cache_len, draft_len = operands
    score_scale = HEAD_DIM ** -0.5
    cache_scores = jnp.einsum("qkgd,lkd->kgql", queries_one.astype(jnp.float32), cache_k.astype(jnp.float32)) * score_scale
    draft_scores = jnp.einsum("qkgd,jkd->kgqj", queries_one.astype(jnp.float32), draft_k.astype(jnp.float32)) * score_scale
    cache_pos = jnp.arange(cache_k.shape[0], dtype=jnp.int32)
    draft_pos = jnp.arange(draft_k.shape[0], dtype=jnp.int32)
    keep_cache = cache_pos < cache_len
    keep_draft = (draft_pos[None, :] <= draft_pos[:, None]) & (draft_pos[None, :] < draft_len)
    cache_scores = jnp.where(keep_cache, cache_scores, NEG_FILL)
    draft_scores = jnp.where(keep_draft, draft_scores, NEG_FILL)
    highest = jnp.maximum(jnp.max(cache_scores, axis=-1, keepdims=True), jnp.max(draft_scores, axis=-1, keepdims=True))
    cache_exp = jnp.exp(cache_scores - highest)
    draft_exp = jnp.exp(draft_scores - highest)
    denominator = jnp.sum(cache_exp, axis=-1, keepdims=True) + jnp.sum(draft_exp, axis=-1, keepdims=True)
    cache_weights = (cache_exp / denominator).astype(jnp.bfloat16)
    draft_weights = (draft_exp / denominator).astype(jnp.bfloat16)
    mixed = jnp.einsum("kgql,lkd->qkgd", cache_weights.astype(jnp.float32), cache_v.astype(jnp.float32))
    mixed = mixed + jnp.einsum("kgqj,jkd->qkgd", draft_weights.astype(jnp.float32), draft_v.astype(jnp.float32))
    is_live = draft_pos < draft_len
    return jnp.where(is_live[:, None, None, None], mixed, 0.0).astype(jnp.bfloat16)


def reference(queries, draft_keys, draft_values, cache_keys, cache_values, out_weight, cache_lengths, draft_lengths, dest_group, dest_offset):
    group_heads = HEADS // KV_HEADS
    query_blocks = queries.reshape(REQUESTS, DRAFT, KV_HEADS, group_heads, HEAD_DIM)
    cache_k = cache_keys.reshape(REQUESTS, CACHE, KV_HEADS, HEAD_DIM)
    cache_v = cache_values.reshape(REQUESTS, CACHE, KV_HEADS, HEAD_DIM)
    draft_k = draft_keys.reshape(REQUESTS, DRAFT, KV_HEADS, HEAD_DIM)
    draft_v = draft_values.reshape(REQUESTS, DRAFT, KV_HEADS, HEAD_DIM)
    attended = lax.map(attend_request, (query_blocks, cache_k, cache_v, draft_k, draft_v, cache_lengths, draft_lengths))
    attended_rows = attended.reshape(REQUESTS * DRAFT, HEADS * HEAD_DIM)
    row_ids = jnp.arange(ROWS, dtype=jnp.int32)
    request, within, is_live = packed_sources(row_ids, draft_lengths, dest_group, dest_offset)
    row_index = (request * DRAFT + within).astype(jnp.int32)
    packed = jnp.where(is_live[:, None], jnp.take(attended_rows, row_index, axis=0), jnp.zeros((), jnp.bfloat16))
    block_width = HEADS * HEAD_DIM // N_TENSOR

    def add_block(index, running):
        first_col = (index * block_width).astype(jnp.int32)
        columns = lax.dynamic_slice_in_dim(packed, first_col, block_width, 1)
        weight_rows = lax.dynamic_slice_in_dim(out_weight, first_col, block_width, 0)
        partial_value = jnp.dot(columns, weight_rows, preferred_element_type=jnp.float32).astype(jnp.bfloat16)
        partial_value = lax.optimization_barrier(partial_value)
        return running + partial_value.astype(jnp.float32)

    running = lax.fori_loop(0, N_TENSOR, add_block, jnp.zeros((ROWS, MODEL_DIM), jnp.float32))
    return running.astype(jnp.bfloat16)
```

```python
import functools
import math

import jax
import jax.numpy as jnp
from jax import lax
from jax.experimental import pallas as pl
from jax.experimental.pallas import tpu as pltpu
from jax.sharding import PartitionSpec as P

HEADS = 128
KV_HEADS = 8
HEAD_DIM = 128
DRAFT = 64
GROUP_REQ = 2
PACK = 96
NEG_FILL = -1e30
MESH = pl.DeviceIdType.MESH
AHEAD = 2


def kernel(
    dp_count,
    tensor_count,
    q_ref,
    dk_ref,
    dv_ref,
    ck_ref,
    cv_ref,
    w_ref,
    clen_ref,
    dlen_ref,
    dgroup_ref,
    doffset_ref,
    o_ref,
    kbuf,
    vbuf,
    wbuf,
    home,
    packed,
    acc,
    own,
    from_left,
    from_right,
    local_sem,
    w_sem,
    kv_send,
    kv_recv,
    ag_send,
    ag_recv,
    fw_send,
    fw_recv,
    rs_send,
    rs_recv,
):
    D, T = dp_count, tensor_count
    half = D // 2
    me = lax.axis_index("dp")
    rank = lax.axis_index("tensor")
    place, parity = me // 2, me % 2
    sibling = me + 1 - 2 * parity
    kv_local = kbuf.shape[0]
    span = ck_ref.shape[1]
    cache = kbuf.shape[2]
    width = packed.shape[2]
    per_kv = width // HEAD_DIM
    local_heads = per_kv * kv_local
    group_heads = HEADS // KV_HEADS
    block_rows = own.shape[1]
    out_cols = own.shape[2]
    tile = min(512, out_cols)
    tiles = out_cols // tile
    chunks = kv_local * GROUP_REQ
    kv_first = rank * local_heads // group_heads

    def peer(offset):
        return 2 * lax.rem(place + offset + half, half) + parity

    barrier = pltpu.get_barrier_semaphore()
    for o in range(1, T):
        pl.semaphore_signal(
            barrier, inc=1, device_id=(me, lax.rem(rank + o, T)), device_id_type=MESH
        )
    for o in range(1, half):
        pl.semaphore_signal(barrier, inc=1, device_id=(peer(o), rank), device_id_type=MESH)
    pl.semaphore_signal(barrier, inc=1, device_id=(sibling, rank), device_id_type=MESH)
    pl.semaphore_wait(barrier, T - 1 + half)

    sources = ((ck_ref, kbuf), (cv_ref, vbuf))

    def kv_copy(c, o, which):
        k, b = divmod(c, GROUP_REQ)
        target = lax.rem(rank + o, T)
        head = target * local_heads // group_heads + k
        src, dst = sources[which]
        return pltpu.make_async_remote_copy(
            src_ref=src.at[b, :, pl.ds(pl.multiple_of(head * HEAD_DIM, HEAD_DIM), HEAD_DIM)],
            dst_ref=dst.at[k, b, pl.ds(pl.multiple_of(rank * span, span), span), :],
            send_sem=kv_send.at[c, o, which],
            recv_sem=kv_recv.at[c, o, which],
            device_id=(me, target),
            device_id_type=MESH,
        )

    def kv_arrival(c, o, which):
        k, b = divmod(c, GROUP_REQ)
        origin = lax.rem(rank - o + T, T)
        dst = sources[which][1]
        landing = dst.at[k, b, pl.ds(pl.multiple_of(origin * span, span), span), :]
        return pltpu.make_async_remote_copy(
            src_ref=landing,
            dst_ref=landing,
            send_sem=kv_send.at[c, o, which],
            recv_sem=kv_recv.at[c, o, which],
            device_id=(me, origin),
            device_id_type=MESH,
        )

    def kv_local_copy(c, which):
        k, b = divmod(c, GROUP_REQ)
        src, dst = sources[which]
        return pltpu.make_async_copy(
            src.at[
                b, :, pl.ds(pl.multiple_of((kv_first + k) * HEAD_DIM, HEAD_DIM), HEAD_DIM)
            ],
            dst.at[k, b, pl.ds(pl.multiple_of(rank * span, span), span), :],
            local_sem.at[c, which],
        )

    def start_kv(c):
        for which in range(2):
            for o in range(T - 1, 0, -1):
                kv_copy(c, o, which).start()
            kv_local_copy(c, which).start()

    def wait_kv(c):
        for which in range(2):
            for o in range(1, T):
                kv_arrival(c, o, which).wait_recv()
            kv_local_copy(c, which).wait()

    def w_copy(k):
        return pltpu.make_async_copy(
            w_ref.at[pl.ds(k * width, width), :], wbuf.at[k], w_sem.at[k]
        )

    head_block = min(4, per_kv)
    rows = head_block * DRAFT
    rate = HEAD_DIM ** (-0.5) * math.log2(math.e)
    nt = (((1,), (1,)), ((), ()))

    def attend(c):
        k, b = divmod(c, GROUP_REQ)
        cache_len = clen_ref[b]
        draft_len = dlen_ref[me * GROUP_REQ + b]
        pos = lax.broadcasted_iota(jnp.int32, (1, cache), 1)
        bias = jnp.where(pos < cache_len, 0.0, NEG_FILL).astype(jnp.float32)
        slot = lax.rem(lax.broadcasted_iota(jnp.int32, (rows, DRAFT), 0), DRAFT)
        key_slot = lax.broadcasted_iota(jnp.int32, (rows, DRAFT), 1)
        keep = (key_slot <= slot) & (key_slot < draft_len)
        draft_bias = jnp.where(keep, 0.0, NEG_FILL).astype(jnp.float32)
        live_slot = lax.rem(lax.broadcasted_iota(jnp.int32, (rows, HEAD_DIM), 0), DRAFT)
        is_live = live_slot < draft_len
        draft_cols = pl.ds(pl.multiple_of((kv_first + k) * HEAD_DIM, HEAD_DIM), HEAD_DIM)
        draft_rows = pl.ds(b * DRAFT, DRAFT)

        def step(j, carry):
            blocks = []
            for h in range(head_block):
                col = pl.multiple_of((k * per_kv + j * head_block + h) * HEAD_DIM, HEAD_DIM)
                blocks.append(q_ref[draft_rows, pl.ds(col, HEAD_DIM)])
            q = jnp.concatenate(blocks, axis=0)
            s = lax.dot_general(q, kbuf[k, b], nt, preferred_element_type=jnp.float32) + bias
            sd = (
                lax.dot_general(
                    q, dk_ref[draft_rows, draft_cols], nt, preferred_element_type=jnp.float32
                )
                + draft_bias
            )
            m = jnp.maximum(
                jnp.max(s, axis=1, keepdims=True), jnp.max(sd, axis=1, keepdims=True)
            )
            p = jnp.exp2((s - m) * rate)
            pd = jnp.exp2((sd - m) * rate)
            total = jnp.sum(p, axis=1, keepdims=True) + jnp.sum(pd, axis=1, keepdims=True)
            mixed = jnp.dot(
                p.astype(jnp.bfloat16), vbuf[k, b], preferred_element_type=jnp.float32
            ) + jnp.dot(
                pd.astype(jnp.bfloat16),
                dv_ref[draft_rows, draft_cols],
                preferred_element_type=jnp.float32,
            )
            mixed = jnp.where(is_live, mixed / total, 0.0).astype(jnp.bfloat16)
            for h in range(head_block):
                col = pl.multiple_of((j * head_block + h) * HEAD_DIM, HEAD_DIM)
                home[c, me, :, pl.ds(col, HEAD_DIM)] = mixed[h * DRAFT : (h + 1) * DRAFT]
            return carry

        lax.fori_loop(0, per_kv // head_block, step, 0)

    def block_copy(c, origin, target, send, recv):
        return pltpu.make_async_remote_copy(
            src_ref=home.at[c, origin],
            dst_ref=home.at[c, origin],
            send_sem=send,
            recv_sem=recv,
            device_id=(target, rank),
            device_id_type=MESH,
        )

    def ag_copy(c, o):
        target = sibling if o == 0 else peer(o)
        return block_copy(c, me, target, ag_send.at[c, o], ag_recv.at[c, o])

    def ag_arrival(c, o):
        origin = sibling if o == 0 else peer(-o)
        return block_copy(c, origin, origin, ag_send.at[c, o], ag_recv.at[c, o])

    def fw_copy(c, o):
        return block_copy(c, peer(-o), sibling, fw_send.at[c, o], fw_recv.at[c, o])

    def fw_arrival(c, o):
        origin = peer(-o) + 1 - 2 * parity
        return block_copy(c, origin, sibling, fw_send.at[c, o], fw_recv.at[c, o])

    def start_ag(c):
        for o in range(half - 1, -1, -1):
            ag_copy(c, o).start()

    def finish_ag(c):
        for o in range(1, half):
            ag_arrival(c, o).wait_recv()
            fw_copy(c, o).start()
        ag_arrival(c, 0).wait_recv()
        for o in range(1, half):
            fw_arrival(c, o).wait_recv()

    source_rows = D * DRAFT

    def pack(c):
        b = c % GROUP_REQ
        column = lax.broadcasted_iota(jnp.int32, (1, source_rows), 1)
        group, slot = column // DRAFT, lax.rem(column, DRAFT)
        goal = jnp.full((1, source_rows), -1, jnp.int32)
        for g in range(D):
            r = g * GROUP_REQ + b
            first = dgroup_ref[r] * PACK + doffset_ref[r]
            goal = jnp.where((group == g) & (slot < dlen_ref[r]), slot + first, goal)

        def step(t, carry):
            row = lax.broadcasted_iota(jnp.int32, (block_rows, source_rows), 0)
            chosen = jnp.where(row + t * block_rows == goal, 1.0, 0.0).astype(jnp.bfloat16)
            got = jnp.dot(
                chosen,
                home[c].reshape(source_rows, width),
                preferred_element_type=jnp.float32,
            )
            if b == 0:
                packed[t] = got.astype(jnp.bfloat16)
            else:
                packed[t] = (packed[t].astype(jnp.float32) + got).astype(jnp.bfloat16)
            return carry

        lax.fori_loop(0, T, step, 0)

    def project(k):
        w_copy(k).wait()

        def step(i, carry):
            t, n = i // tiles, lax.rem(i, tiles)
            cols = pl.ds(pl.multiple_of(n * tile, tile), tile)
            part = jnp.dot(packed[t], wbuf[k, :, cols], preferred_element_type=jnp.float32)
            if k > 0:
                part = part + acc[t, :, cols]
            acc[t, :, cols] = part
            return carry

        lax.fori_loop(0, T * tiles, step, 0)

    def piece(n):
        return pl.ds(pl.multiple_of(n * tile, tile), tile)

    def rs_copy(direction, s, n):
        landing = from_left if direction == 0 else from_right
        target = rank + 1 if direction == 0 else rank - 1
        return pltpu.make_async_remote_copy(
            src_ref=own.at[s, :, piece(n)],
            dst_ref=landing.at[s, :, piece(n)],
            send_sem=rs_send.at[direction, s, n],
            recv_sem=rs_recv.at[direction, s, n],
            device_id=(me, target),
            device_id_type=MESH,
        )

    def rs_arrival(direction, s, n):
        landing = from_left if direction == 0 else from_right
        place_at = landing.at[s, :, piece(n)]
        origin = rank - 1 if direction == 0 else rank + 1
        return pltpu.make_async_remote_copy(
            src_ref=place_at,
            dst_ref=place_at,
            send_sem=rs_send.at[direction, s, n],
            recv_sem=rs_recv.at[direction, s, n],
            device_id=(me, origin),
            device_id_type=MESH,
        )

    def project_last(k):
        w_copy(k).wait()

        def step(i, carry):
            order, n = i // tiles, lax.rem(i, tiles)
            depth = order // 2
            s = jnp.where(lax.rem(order, 2) == 0, T - 1 - depth, depth)
            cols = piece(n)
            part = jnp.dot(packed[s], wbuf[k, :, cols], preferred_element_type=jnp.float32)
            if k > 0:
                part = part + acc[s, :, cols]
            own[s, :, cols] = part.astype(jnp.bfloat16)

            @pl.when((rank == 0) & (s > 0))
            def _():
                rs_copy(0, s, n).start()

            @pl.when((rank == T - 1) & (s < T - 1))
            def _():
                rs_copy(1, s, n).start()

            return carry

        lax.fori_loop(0, T * tiles, step, 0)

    def relay(i, carry):
        order, n = i // tiles, lax.rem(i, tiles)
        cols = piece(n)
        s_right, s_left = T - 1 - order, order

        @pl.when((rank > 0) & (s_right > rank))
        def _():
            rs_arrival(0, s_right, n).wait_recv()
            own[s_right, :, cols] = (
                own[s_right, :, cols].astype(jnp.float32)
                + from_left[s_right, :, cols].astype(jnp.float32)
            ).astype(jnp.bfloat16)
            rs_copy(0, s_right, n).start()

        @pl.when((rank < T - 1) & (s_left < rank))
        def _():
            rs_arrival(1, s_left, n).wait_recv()
            own[s_left, :, cols] = (
                own[s_left, :, cols].astype(jnp.float32)
                + from_right[s_left, :, cols].astype(jnp.float32)
            ).astype(jnp.bfloat16)
            rs_copy(1, s_left, n).start()

        return carry

    def settle(n, carry):
        cols = piece(n)
        acc[0, :, cols] = own[rank, :, cols].astype(jnp.float32)

        @pl.when(rank > 0)
        def _():
            rs_arrival(0, rank, n).wait_recv()
            acc[0, :, cols] = acc[0, :, cols] + from_left[rank, :, cols].astype(jnp.float32)

        @pl.when(rank < T - 1)
        def _():
            rs_arrival(1, rank, n).wait_recv()
            acc[0, :, cols] = acc[0, :, cols] + from_right[rank, :, cols].astype(jnp.float32)

        o_ref[:, cols] = acc[0, :, cols].astype(jnp.bfloat16)
        return carry

    def drain(i, carry):
        s, n = i // tiles, lax.rem(i, tiles)

        @pl.when(s > rank)
        def _():
            rs_copy(0, s, n).wait_send()

        @pl.when(s < rank)
        def _():
            rs_copy(1, s, n).wait_send()

        return carry

    for c in range(min(AHEAD, chunks)):
        start_kv(c)
    for k in range(kv_local):
        w_copy(k).start()

    def absorb(c):
        k, b = divmod(c, GROUP_REQ)
        finish_ag(c)
        pack(c)
        if b == GROUP_REQ - 1:
            if k == kv_local - 1:
                project_last(k)
            else:
                project(k)

    for c in range(chunks):
        wait_kv(c)
        if c + AHEAD < chunks:
            start_kv(c + AHEAD)
        attend(c)
        start_ag(c)
        if c > 0:
            absorb(c - 1)
    absorb(chunks - 1)
    lax.fori_loop(0, T * tiles, relay, 0)
    lax.fori_loop(0, tiles, settle, 0)
    lax.fori_loop(0, T * tiles, drain, 0)
    for c in range(chunks):
        for which in range(2):
            for o in range(1, T):
                kv_copy(c, o, which).wait_send()
        for o in range(half):
            ag_copy(c, o).wait_send()
        for o in range(1, half):
            fw_copy(c, o).wait_send()


def body(
    queries,
    draft_keys,
    draft_values,
    cache_keys,
    cache_values,
    out_weight,
    cache_lengths,
    draft_lengths,
    dest_group,
    dest_offset,
):
    T = lax.axis_size("tensor")
    D = lax.axis_size("dp")
    local_heads = HEADS // T
    group_heads = HEADS // KV_HEADS
    kv_local = max(1, local_heads // group_heads)
    width = local_heads // kv_local * HEAD_DIM
    cache = cache_keys.shape[1] * T
    out_cols = out_weight.shape[1]
    block_rows = PACK * D // T
    tiles = out_cols // min(512, out_cols)
    chunks = kv_local * GROUP_REQ
    half = D // 2
    vmem = pl.BlockSpec(memory_space=pltpu.VMEM)
    smem = pl.BlockSpec(memory_space=pltpu.SMEM)
    anywhere = pl.BlockSpec(memory_space=pl.ANY)
    dma = pltpu.SemaphoreType.DMA
    bf16 = jnp.bfloat16
    return pl.pallas_call(
        functools.partial(kernel, D, T),
        out_shape=jax.ShapeDtypeStruct((block_rows, out_cols), bf16),
        in_specs=[vmem] * 3 + [anywhere] * 3 + [smem] * 4,
        out_specs=vmem,
        scratch_shapes=[
            pltpu.VMEM((kv_local, GROUP_REQ, cache, HEAD_DIM), bf16),
            pltpu.VMEM((kv_local, GROUP_REQ, cache, HEAD_DIM), bf16),
            pltpu.VMEM((kv_local, width, out_cols), bf16),
            pltpu.VMEM((chunks, D, DRAFT, width), bf16),
            pltpu.VMEM((T, block_rows, width), bf16),
            pltpu.VMEM((T, block_rows, out_cols), jnp.float32),
            pltpu.VMEM((T, block_rows, out_cols), bf16),
            pltpu.VMEM((T, block_rows, out_cols), bf16),
            pltpu.VMEM((T, block_rows, out_cols), bf16),
            dma((chunks, 2)),
            dma((kv_local,)),
            dma((chunks, T, 2)),
            dma((chunks, T, 2)),
            dma((chunks, half)),
            dma((chunks, half)),
            dma((chunks, half)),
            dma((chunks, half)),
            dma((2, T, tiles)),
            dma((2, T, tiles)),
        ],
        compiler_params=pltpu.CompilerParams(
            collective_id=0, has_side_effects=True, vmem_limit_bytes=60 * 2**20
        ),
    )(
        queries,
        draft_keys,
        draft_values,
        cache_keys,
        cache_values,
        out_weight,
        cache_lengths,
        draft_lengths,
        dest_group,
        dest_offset,
    )


def solution(mesh):
    in_specs = (
        P("dp", "tensor"),
        P("dp", None),
        P("dp", None),
        P("dp", "tensor", None),
        P("dp", "tensor", None),
        P("tensor", "dp"),
        P("dp"),
        P(),
        P(),
        P(),
    )
    out_specs = P("tensor", "dp")
    return jax.shard_map(body, mesh=mesh, in_specs=in_specs, out_specs=out_specs, check_vma=False)
```

```python
import functools
import math

import jax
import jax.numpy as jnp
from jax import lax
from jax.experimental import pallas as pl
from jax.experimental.pallas import tpu as pltpu
from jax.sharding import PartitionSpec as P

HEADS = 128
KV_HEADS = 8
HEAD_DIM = 128
DRAFT = 64
GROUP_REQ = 2
PACK = 96
NEG_FILL = -1e30
MESH = pl.DeviceIdType.MESH
SLAB = 768


def kernel(
    dp_count,
    tensor_count,
    q_ref,
    dk_ref,
    dv_ref,
    ck_ref,
    cv_ref,
    w_ref,
    clen_ref,
    dlen_ref,
    dgroup_ref,
    doffset_ref,
    o_ref,
    kbuf,
    vbuf,
    wbuf,
    home,
    weights,
    totals,
    draft_part,
    packed,
    acc,
    own,
    from_left,
    from_right,
    local_sem,
    w_sem,
    kv_send,
    kv_recv,
    ag_send,
    ag_recv,
    fw_send,
    fw_recv,
    rs_send,
    rs_recv,
):
    D, T = dp_count, tensor_count
    half = D // 2
    me = lax.axis_index("dp")
    rank = lax.axis_index("tensor")
    place, parity = me // 2, me % 2
    sibling = me + 1 - 2 * parity
    kv_local = kbuf.shape[0]
    span = ck_ref.shape[1]
    cache = kbuf.shape[2]
    width = packed.shape[1]
    per_kv = width // HEAD_DIM
    local_heads = per_kv * kv_local
    group_heads = HEADS // KV_HEADS
    all_rows, out_cols = own.shape
    block_rows = all_rows // T
    slab = min(SLAB, all_rows)
    slabs = all_rows // slab
    tile = min(512, out_cols)
    tiles = out_cols // tile
    chunks = kv_local * GROUP_REQ
    kv_first = rank * local_heads // group_heads

    def peer(offset):
        return 2 * lax.rem(place + offset + half, half) + parity

    barrier = pltpu.get_barrier_semaphore()
    for o in range(1, T):
        pl.semaphore_signal(
            barrier, inc=1, device_id=(me, lax.rem(rank + o, T)), device_id_type=MESH
        )
    for o in range(1, half):
        pl.semaphore_signal(barrier, inc=1, device_id=(peer(o), rank), device_id_type=MESH)
    pl.semaphore_signal(barrier, inc=1, device_id=(sibling, rank), device_id_type=MESH)
    pl.semaphore_wait(barrier, T - 1 + half)

    sources = ((ck_ref, kbuf), (cv_ref, vbuf))

    def kv_copy(c, o, which):
        k, b = divmod(c, GROUP_REQ)
        target = lax.rem(rank + o, T)
        head = target * local_heads // group_heads + k
        src, dst = sources[which]
        return pltpu.make_async_remote_copy(
            src_ref=src.at[b, :, pl.ds(pl.multiple_of(head * HEAD_DIM, HEAD_DIM), HEAD_DIM)],
            dst_ref=dst.at[k, b, pl.ds(pl.multiple_of(rank * span, span), span), :],
            send_sem=kv_send.at[c, o, which],
            recv_sem=kv_recv.at[c, o, which],
            device_id=(me, target),
            device_id_type=MESH,
        )

    def kv_arrival(c, o, which):
        k, b = divmod(c, GROUP_REQ)
        origin = lax.rem(rank - o + T, T)
        dst = sources[which][1]
        landing = dst.at[k, b, pl.ds(pl.multiple_of(origin * span, span), span), :]
        return pltpu.make_async_remote_copy(
            src_ref=landing,
            dst_ref=landing,
            send_sem=kv_send.at[c, o, which],
            recv_sem=kv_recv.at[c, o, which],
            device_id=(me, origin),
            device_id_type=MESH,
        )

    def kv_local_copy(c, which):
        k, b = divmod(c, GROUP_REQ)
        src, dst = sources[which]
        return pltpu.make_async_copy(
            src.at[
                b, :, pl.ds(pl.multiple_of((kv_first + k) * HEAD_DIM, HEAD_DIM), HEAD_DIM)
            ],
            dst.at[k, b, pl.ds(pl.multiple_of(rank * span, span), span), :],
            local_sem.at[c, which],
        )

    def start_kv(c, which):
        for o in range(T - 1, 0, -1):
            kv_copy(c, o, which).start()
        kv_local_copy(c, which).start()

    def wait_kv(c, which):
        for o in range(1, T):
            kv_arrival(c, o, which).wait_recv()
        kv_local_copy(c, which).wait()

    def w_copy(k):
        return pltpu.make_async_copy(
            w_ref.at[pl.ds(k * width, width), :], wbuf.at[k], w_sem.at[k]
        )

    head_block = min(4, per_kv)
    rows = head_block * DRAFT
    rate = HEAD_DIM ** (-0.5) * math.log2(math.e)
    nt = (((1,), (1,)), ((), ()))

    def score(c):
        k, b = divmod(c, GROUP_REQ)
        cache_len = clen_ref[b]
        draft_len = dlen_ref[me * GROUP_REQ + b]
        pos = lax.broadcasted_iota(jnp.int32, (1, cache), 1)
        bias = jnp.where(pos < cache_len, 0.0, NEG_FILL).astype(jnp.float32)
        slot = lax.rem(lax.broadcasted_iota(jnp.int32, (rows, DRAFT), 0), DRAFT)
        key_slot = lax.broadcasted_iota(jnp.int32, (rows, DRAFT), 1)
        keep = (key_slot <= slot) & (key_slot < draft_len)
        draft_bias = jnp.where(keep, 0.0, NEG_FILL).astype(jnp.float32)
        draft_cols = pl.ds(pl.multiple_of((kv_first + k) * HEAD_DIM, HEAD_DIM), HEAD_DIM)
        draft_rows = pl.ds(b * DRAFT, DRAFT)

        def step(j, carry):
            blocks = []
            for h in range(head_block):
                col = pl.multiple_of((k * per_kv + j * head_block + h) * HEAD_DIM, HEAD_DIM)
                blocks.append(q_ref[draft_rows, pl.ds(col, HEAD_DIM)])
            q = jnp.concatenate(blocks, axis=0)
            s = lax.dot_general(q, kbuf[k, b], nt, preferred_element_type=jnp.float32) + bias
            sd = (
                lax.dot_general(
                    q, dk_ref[draft_rows, draft_cols], nt, preferred_element_type=jnp.float32
                )
                + draft_bias
            )
            m = jnp.maximum(
                jnp.max(s, axis=1, keepdims=True), jnp.max(sd, axis=1, keepdims=True)
            )
            p = jnp.exp2((s - m) * rate)
            pd = jnp.exp2((sd - m) * rate)
            at = pl.ds(pl.multiple_of(j * rows, rows), rows)
            total = jnp.sum(p, axis=1, keepdims=True) + jnp.sum(pd, axis=1, keepdims=True)
            totals[at, :] = jnp.broadcast_to(total, (rows, HEAD_DIM))
            weights[at, :] = p.astype(jnp.bfloat16)
            draft_part[at, :] = jnp.dot(
                pd.astype(jnp.bfloat16),
                dv_ref[draft_rows, draft_cols],
                preferred_element_type=jnp.float32,
            )
            return carry

        lax.fori_loop(0, per_kv // head_block, step, 0)

    def mix(c):
        k, b = divmod(c, GROUP_REQ)
        draft_len = dlen_ref[me * GROUP_REQ + b]
        live_slot = lax.rem(lax.broadcasted_iota(jnp.int32, (rows, HEAD_DIM), 0), DRAFT)
        is_live = live_slot < draft_len

        def step(j, carry):
            at = pl.ds(pl.multiple_of(j * rows, rows), rows)
            mixed = (
                jnp.dot(weights[at, :], vbuf[k, b], preferred_element_type=jnp.float32)
                + draft_part[at, :]
            )
            mixed = jnp.where(is_live, mixed / totals[at, :], 0.0).astype(jnp.bfloat16)
            for h in range(head_block):
                col = pl.multiple_of((j * head_block + h) * HEAD_DIM, HEAD_DIM)
                home[c, me, :, pl.ds(col, HEAD_DIM)] = mixed[h * DRAFT : (h + 1) * DRAFT]
            return carry

        lax.fori_loop(0, per_kv // head_block, step, 0)

    def block_copy(c, origin, target, send, recv):
        return pltpu.make_async_remote_copy(
            src_ref=home.at[c, origin],
            dst_ref=home.at[c, origin],
            send_sem=send,
            recv_sem=recv,
            device_id=(target, rank),
            device_id_type=MESH,
        )

    def ag_copy(c, o):
        target = sibling if o == 0 else peer(o)
        return block_copy(c, me, target, ag_send.at[c, o], ag_recv.at[c, o])

    def ag_arrival(c, o):
        origin = sibling if o == 0 else peer(-o)
        return block_copy(c, origin, origin, ag_send.at[c, o], ag_recv.at[c, o])

    def fw_copy(c, o):
        return block_copy(c, peer(-o), sibling, fw_send.at[c, o], fw_recv.at[c, o])

    def fw_arrival(c, o):
        origin = peer(-o) + 1 - 2 * parity
        return block_copy(c, origin, sibling, fw_send.at[c, o], fw_recv.at[c, o])

    def start_ag(c):
        for o in range(half - 1, -1, -1):
            ag_copy(c, o).start()

    def finish_ag(c):
        for o in range(1, half):
            ag_arrival(c, o).wait_recv()
            fw_copy(c, o).start()
        ag_arrival(c, 0).wait_recv()
        for o in range(1, half):
            fw_arrival(c, o).wait_recv()

    source_rows = D * DRAFT

    def pack(c):
        b = c % GROUP_REQ
        column = lax.broadcasted_iota(jnp.int32, (1, source_rows), 1)
        group, slot = column // DRAFT, lax.rem(column, DRAFT)
        goal = jnp.full((1, source_rows), -1, jnp.int32)
        for g in range(D):
            r = g * GROUP_REQ + b
            first = dgroup_ref[r] * PACK + doffset_ref[r]
            goal = jnp.where((group == g) & (slot < dlen_ref[r]), slot + first, goal)

        pack_tile = min(512, width)

        def slab_step(t, carry):
            at = pl.ds(pl.multiple_of(t * slab, slab), slab)
            row = lax.broadcasted_iota(jnp.int32, (slab, source_rows), 0)
            chosen = jnp.where(row + t * slab == goal, 1.0, 0.0).astype(jnp.bfloat16)

            def step(n, carry):
                cols = pl.ds(pl.multiple_of(n * pack_tile, pack_tile), pack_tile)
                got = jnp.dot(
                    chosen,
                    home[c, :, :, cols].reshape(source_rows, pack_tile),
                    preferred_element_type=jnp.float32,
                )
                if b > 0:
                    got = got + packed[at, cols].astype(jnp.float32)
                packed[at, cols] = got.astype(jnp.bfloat16)
                return carry

            return lax.fori_loop(0, width // pack_tile, step, carry)

        lax.fori_loop(0, slabs, slab_step, 0)

    def project(k):
        w_copy(k).wait()

        def step(i, carry):
            n, t = i // slabs, lax.rem(i, slabs)
            cols = pl.ds(pl.multiple_of(n * tile, tile), tile)
            at = pl.ds(pl.multiple_of(t * slab, slab), slab)
            part = jnp.dot(packed[at, :], wbuf[k, :, cols], preferred_element_type=jnp.float32)
            if k > 0:
                part = part + acc[at, cols]
            acc[at, cols] = part
            return carry

        lax.fori_loop(0, slabs * tiles, step, 0)

    def block(s):
        return pl.ds(pl.multiple_of(s * block_rows, block_rows), block_rows)

    def piece(n):
        return pl.ds(pl.multiple_of(n * tile, tile), tile)

    def rs_copy(direction, s, n):
        landing = from_left if direction == 0 else from_right
        target = rank + 1 if direction == 0 else rank - 1
        return pltpu.make_async_remote_copy(
            src_ref=own.at[block(s), piece(n)],
            dst_ref=landing.at[block(s), piece(n)],
            send_sem=rs_send.at[direction, s, n],
            recv_sem=rs_recv.at[direction, s, n],
            device_id=(me, target),
            device_id_type=MESH,
        )

    def rs_arrival(direction, s, n):
        landing = from_left if direction == 0 else from_right
        place_at = landing.at[block(s), piece(n)]
        origin = rank - 1 if direction == 0 else rank + 1
        return pltpu.make_async_remote_copy(
            src_ref=place_at,
            dst_ref=place_at,
            send_sem=rs_send.at[direction, s, n],
            recv_sem=rs_recv.at[direction, s, n],
            device_id=(me, origin),
            device_id_type=MESH,
        )

    def project_last(k):
        w_copy(k).wait()

        def step(n, carry):
            cols = piece(n)
            for t in range(slabs):
                at = pl.ds(t * slab, slab)
                part = jnp.dot(
                    packed[at, :], wbuf[k, :, cols], preferred_element_type=jnp.float32
                )
                if k > 0:
                    part = part + acc[at, cols]
                own[at, cols] = part.astype(jnp.bfloat16)

            @pl.when(rank == 0)
            def _():
                for s in range(T - 1, 0, -1):
                    rs_copy(0, s, n).start()

            @pl.when(rank == T - 1)
            def _():
                for s in range(T - 1):
                    rs_copy(1, s, n).start()

            return carry

        lax.fori_loop(0, tiles, step, 0)

    def relay(i, carry):
        n, order = i // T, lax.rem(i, T)
        cols = piece(n)
        s_right, s_left = T - 1 - order, order

        @pl.when((rank > 0) & (s_right > rank))
        def _():
            rs_arrival(0, s_right, n).wait_recv()
            own[block(s_right), cols] = (
                own[block(s_right), cols].astype(jnp.float32)
                + from_left[block(s_right), cols].astype(jnp.float32)
            ).astype(jnp.bfloat16)
            rs_copy(0, s_right, n).start()

        @pl.when((rank < T - 1) & (s_left < rank))
        def _():
            rs_arrival(1, s_left, n).wait_recv()
            own[block(s_left), cols] = (
                own[block(s_left), cols].astype(jnp.float32)
                + from_right[block(s_left), cols].astype(jnp.float32)
            ).astype(jnp.bfloat16)
            rs_copy(1, s_left, n).start()

        return carry

    def settle(n, carry):
        cols = piece(n)
        acc[:block_rows, cols] = own[block(rank), cols].astype(jnp.float32)

        @pl.when(rank > 0)
        def _():
            rs_arrival(0, rank, n).wait_recv()
            acc[:block_rows, cols] = acc[:block_rows, cols] + from_left[block(rank), cols].astype(jnp.float32)

        @pl.when(rank < T - 1)
        def _():
            rs_arrival(1, rank, n).wait_recv()
            acc[:block_rows, cols] = acc[:block_rows, cols] + from_right[block(rank), cols].astype(jnp.float32)

        o_ref[:, cols] = acc[:block_rows, cols].astype(jnp.bfloat16)
        return carry

    def drain(i, carry):
        s, n = i // tiles, lax.rem(i, tiles)

        @pl.when(s > rank)
        def _():
            rs_copy(0, s, n).wait_send()

        @pl.when(s < rank)
        def _():
            rs_copy(1, s, n).wait_send()

        return carry

    for which in range(2):
        start_kv(0, which)
    for k in range(kv_local):
        w_copy(k).start()

    def absorb(c):
        k, b = divmod(c, GROUP_REQ)
        finish_ag(c)
        pack(c)
        if b == GROUP_REQ - 1:
            if k == kv_local - 1:
                project_last(k)
            else:
                project(k)

    for c in range(chunks):
        wait_kv(c, 0)
        if c + 1 < chunks:
            start_kv(c + 1, 0)
        score(c)
        if c > 0:
            absorb(c - 1)
        wait_kv(c, 1)
        if c + 1 < chunks:
            start_kv(c + 1, 1)
        mix(c)
        start_ag(c)
    absorb(chunks - 1)
    lax.fori_loop(0, T * tiles, relay, 0)
    lax.fori_loop(0, tiles, settle, 0)
    lax.fori_loop(0, T * tiles, drain, 0)
    for c in range(chunks):
        for which in range(2):
            for o in range(1, T):
                kv_copy(c, o, which).wait_send()
        for o in range(half):
            ag_copy(c, o).wait_send()
        for o in range(1, half):
            fw_copy(c, o).wait_send()


def body(
    queries,
    draft_keys,
    draft_values,
    cache_keys,
    cache_values,
    out_weight,
    cache_lengths,
    draft_lengths,
    dest_group,
    dest_offset,
):
    T = lax.axis_size("tensor")
    D = lax.axis_size("dp")
    local_heads = HEADS // T
    group_heads = HEADS // KV_HEADS
    kv_local = max(1, local_heads // group_heads)
    width = local_heads // kv_local * HEAD_DIM
    cache = cache_keys.shape[1] * T
    out_cols = out_weight.shape[1]
    block_rows = PACK * D // T
    tiles = out_cols // min(512, out_cols)
    chunks = kv_local * GROUP_REQ
    half = D // 2
    vmem = pl.BlockSpec(memory_space=pltpu.VMEM)
    smem = pl.BlockSpec(memory_space=pltpu.SMEM)
    anywhere = pl.BlockSpec(memory_space=pl.ANY)
    dma = pltpu.SemaphoreType.DMA
    bf16 = jnp.bfloat16
    return pl.pallas_call(
        functools.partial(kernel, D, T),
        out_shape=jax.ShapeDtypeStruct((block_rows, out_cols), bf16),
        in_specs=[vmem] * 3 + [anywhere] * 3 + [smem] * 4,
        out_specs=vmem,
        scratch_shapes=[
            pltpu.VMEM((kv_local, GROUP_REQ, cache, HEAD_DIM), bf16),
            pltpu.VMEM((kv_local, GROUP_REQ, cache, HEAD_DIM), bf16),
            pltpu.VMEM((kv_local, width, out_cols), bf16),
            pltpu.VMEM((chunks, D, DRAFT, width), bf16),
            pltpu.VMEM((width // HEAD_DIM * DRAFT, cache), bf16),
            pltpu.VMEM((width // HEAD_DIM * DRAFT, HEAD_DIM), jnp.float32),
            pltpu.VMEM((width // HEAD_DIM * DRAFT, HEAD_DIM), jnp.float32),
            pltpu.VMEM((T * block_rows, width), bf16),
            pltpu.VMEM((T * block_rows, out_cols), jnp.float32),
            pltpu.VMEM((T * block_rows, out_cols), bf16),
            pltpu.VMEM((T * block_rows, out_cols), bf16),
            pltpu.VMEM((T * block_rows, out_cols), bf16),
            dma((chunks, 2)),
            dma((kv_local,)),
            dma((chunks, T, 2)),
            dma((chunks, T, 2)),
            dma((chunks, half)),
            dma((chunks, half)),
            dma((chunks, half)),
            dma((chunks, half)),
            dma((2, T, tiles)),
            dma((2, T, tiles)),
        ],
        compiler_params=pltpu.CompilerParams(
            collective_id=0, has_side_effects=True, vmem_limit_bytes=60 * 2**20
        ),
    )(
        queries,
        draft_keys,
        draft_values,
        cache_keys,
        cache_values,
        out_weight,
        cache_lengths,
        draft_lengths,
        dest_group,
        dest_offset,
    )


def solution(mesh):
    in_specs = (
        P("dp", "tensor"),
        P("dp", None),
        P("dp", None),
        P("dp", "tensor", None),
        P("dp", "tensor", None),
        P("tensor", "dp"),
        P("dp"),
        P(),
        P(),
        P(),
    )
    out_specs = P("tensor", "dp")
    return jax.shard_map(body, mesh=mesh, in_specs=in_specs, out_specs=out_specs, check_vma=False)
```

```python
import functools
import math

import jax
import jax.numpy as jnp
from jax import lax
from jax.experimental import pallas as pl
from jax.experimental.pallas import tpu as pltpu
from jax.sharding import PartitionSpec as P

HEADS = 128
KV_HEADS = 8
HEAD_DIM = 128
DRAFT = 64
GROUP_REQ = 2
PACK = 96
NEG_FILL = -1e30
MESH = pl.DeviceIdType.MESH
AHEAD = 1


def kernel(
    dp_count,
    tensor_count,
    q_ref,
    dk_ref,
    dv_ref,
    ck_ref,
    cv_ref,
    w_ref,
    clen_ref,
    dlen_ref,
    dgroup_ref,
    doffset_ref,
    o_ref,
    kbuf,
    vbuf,
    wbuf,
    home,
    packed,
    acc,
    own,
    from_left,
    from_right,
    local_sem,
    w_sem,
    kv_send,
    kv_recv,
    ag_send,
    ag_recv,
    fw_send,
    fw_recv,
    rs_send,
    rs_recv,
):
    D, T = dp_count, tensor_count
    half = D // 2
    me = lax.axis_index("dp")
    rank = lax.axis_index("tensor")
    place, parity = me // 2, me % 2
    sibling = me + 1 - 2 * parity
    kv_local = kbuf.shape[0]
    span = ck_ref.shape[1]
    cache = kbuf.shape[2]
    width = packed.shape[2]
    per_kv = width // HEAD_DIM
    local_heads = per_kv * kv_local
    group_heads = HEADS // KV_HEADS
    block_rows = own.shape[1]
    out_cols = own.shape[2]
    tile = min(512, out_cols)
    tiles = out_cols // tile
    chunks = kv_local * GROUP_REQ
    kv_first = rank * local_heads // group_heads

    def peer(offset):
        return 2 * lax.rem(place + offset + half, half) + parity

    barrier = pltpu.get_barrier_semaphore()
    for o in range(1, T):
        pl.semaphore_signal(
            barrier, inc=1, device_id=(me, lax.rem(rank + o, T)), device_id_type=MESH
        )
    for o in range(1, half):
        pl.semaphore_signal(barrier, inc=1, device_id=(peer(o), rank), device_id_type=MESH)
    pl.semaphore_signal(barrier, inc=1, device_id=(sibling, rank), device_id_type=MESH)
    pl.semaphore_wait(barrier, T - 1 + half)

    sources = ((ck_ref, kbuf), (cv_ref, vbuf))

    def kv_copy(c, o, which):
        k, b = divmod(c, GROUP_REQ)
        target = lax.rem(rank + o, T)
        head = target * local_heads // group_heads + k
        src, dst = sources[which]
        return pltpu.make_async_remote_copy(
            src_ref=src.at[b, :, pl.ds(pl.multiple_of(head * HEAD_DIM, HEAD_DIM), HEAD_DIM)],
            dst_ref=dst.at[k, b, pl.ds(pl.multiple_of(rank * span, span), span), :],
            send_sem=kv_send.at[c, o, which],
            recv_sem=kv_recv.at[c, o, which],
            device_id=(me, target),
            device_id_type=MESH,
        )

    def kv_arrival(c, o, which):
        k, b = divmod(c, GROUP_REQ)
        origin = lax.rem(rank - o + T, T)
        dst = sources[which][1]
        landing = dst.at[k, b, pl.ds(pl.multiple_of(origin * span, span), span), :]
        return pltpu.make_async_remote_copy(
            src_ref=landing,
            dst_ref=landing,
            send_sem=kv_send.at[c, o, which],
            recv_sem=kv_recv.at[c, o, which],
            device_id=(me, origin),
            device_id_type=MESH,
        )

    def kv_local_copy(c, which):
        k, b = divmod(c, GROUP_REQ)
        src, dst = sources[which]
        return pltpu.make_async_copy(
            src.at[
                b, :, pl.ds(pl.multiple_of((kv_first + k) * HEAD_DIM, HEAD_DIM), HEAD_DIM)
            ],
            dst.at[k, b, pl.ds(pl.multiple_of(rank * span, span), span), :],
            local_sem.at[c, which],
        )

    def start_kv(c):
        for which in range(2):
            for o in range(T - 1, 0, -1):
                kv_copy(c, o, which).start()
            kv_local_copy(c, which).start()

    def wait_kv(c):
        for which in range(2):
            for o in range(1, T):
                kv_arrival(c, o, which).wait_recv()
            kv_local_copy(c, which).wait()

    def w_copy(k):
        return pltpu.make_async_copy(
            w_ref.at[pl.ds(k * width, width), :], wbuf.at[k], w_sem.at[k]
        )

    head_block = min(4, per_kv)
    rows = head_block * DRAFT
    rate = HEAD_DIM ** (-0.5) * math.log2(math.e)
    nt = (((1,), (1,)), ((), ()))

    def attend(c):
        k, b = divmod(c, GROUP_REQ)
        cache_len = clen_ref[b]
        draft_len = dlen_ref[me * GROUP_REQ + b]
        pos = lax.broadcasted_iota(jnp.int32, (1, cache), 1)
        bias = jnp.where(pos < cache_len, 0.0, NEG_FILL).astype(jnp.float32)
        slot = lax.rem(lax.broadcasted_iota(jnp.int32, (rows, DRAFT), 0), DRAFT)
        key_slot = lax.broadcasted_iota(jnp.int32, (rows, DRAFT), 1)
        keep = (key_slot <= slot) & (key_slot < draft_len)
        draft_bias = jnp.where(keep, 0.0, NEG_FILL).astype(jnp.float32)
        live_slot = lax.rem(lax.broadcasted_iota(jnp.int32, (rows, HEAD_DIM), 0), DRAFT)
        is_live = live_slot < draft_len
        draft_cols = pl.ds(pl.multiple_of((kv_first + k) * HEAD_DIM, HEAD_DIM), HEAD_DIM)
        draft_rows = pl.ds(b * DRAFT, DRAFT)

        def step(j, carry):
            blocks = []
            for h in range(head_block):
                col = pl.multiple_of((k * per_kv + j * head_block + h) * HEAD_DIM, HEAD_DIM)
                blocks.append(q_ref[draft_rows, pl.ds(col, HEAD_DIM)])
            q = jnp.concatenate(blocks, axis=0)
            s = lax.dot_general(q, kbuf[k, b], nt, preferred_element_type=jnp.float32) + bias
            sd = (
                lax.dot_general(
                    q, dk_ref[draft_rows, draft_cols], nt, preferred_element_type=jnp.float32
                )
                + draft_bias
            )
            m = jnp.maximum(
                jnp.max(s, axis=1, keepdims=True), jnp.max(sd, axis=1, keepdims=True)
            )
            p = jnp.exp2((s - m) * rate)
            pd = jnp.exp2((sd - m) * rate)
            total = jnp.sum(p, axis=1, keepdims=True) + jnp.sum(pd, axis=1, keepdims=True)
            mixed = jnp.dot(
                p.astype(jnp.bfloat16), vbuf[k, b], preferred_element_type=jnp.float32
            ) + jnp.dot(
                pd.astype(jnp.bfloat16),
                dv_ref[draft_rows, draft_cols],
                preferred_element_type=jnp.float32,
            )
            mixed = jnp.where(is_live, mixed / total, 0.0).astype(jnp.bfloat16)
            for h in range(head_block):
                col = pl.multiple_of((j * head_block + h) * HEAD_DIM, HEAD_DIM)
                home[c, me, :, pl.ds(col, HEAD_DIM)] = mixed[h * DRAFT : (h + 1) * DRAFT]
            return carry

        lax.fori_loop(0, per_kv // head_block, step, 0)

    def block_copy(c, origin, target, send, recv):
        return pltpu.make_async_remote_copy(
            src_ref=home.at[c, origin],
            dst_ref=home.at[c, origin],
            send_sem=send,
            recv_sem=recv,
            device_id=(target, rank),
            device_id_type=MESH,
        )

    def ag_copy(c, o):
        target = sibling if o == 0 else peer(o)
        return block_copy(c, me, target, ag_send.at[c, o], ag_recv.at[c, o])

    def ag_arrival(c, o):
        origin = sibling if o == 0 else peer(-o)
        return block_copy(c, origin, origin, ag_send.at[c, o], ag_recv.at[c, o])

    def fw_copy(c, o):
        return block_copy(c, peer(-o), sibling, fw_send.at[c, o], fw_recv.at[c, o])

    def fw_arrival(c, o):
        origin = peer(-o) + 1 - 2 * parity
        return block_copy(c, origin, sibling, fw_send.at[c, o], fw_recv.at[c, o])

    def start_ag(c):
        for o in range(half - 1, -1, -1):
            ag_copy(c, o).start()

    def finish_ag(c):
        for o in range(1, half):
            ag_arrival(c, o).wait_recv()
            fw_copy(c, o).start()
        ag_arrival(c, 0).wait_recv()
        for o in range(1, half):
            fw_arrival(c, o).wait_recv()

    source_rows = D * DRAFT

    def pack(c):
        b = c % GROUP_REQ
        column = lax.broadcasted_iota(jnp.int32, (1, source_rows), 1)
        group, slot = column // DRAFT, lax.rem(column, DRAFT)
        goal = jnp.full((1, source_rows), -1, jnp.int32)
        for g in range(D):
            r = g * GROUP_REQ + b
            first = dgroup_ref[r] * PACK + doffset_ref[r]
            goal = jnp.where((group == g) & (slot < dlen_ref[r]), slot + first, goal)

        def step(t, carry):
            row = lax.broadcasted_iota(jnp.int32, (block_rows, source_rows), 0)
            chosen = jnp.where(row + t * block_rows == goal, 1.0, 0.0).astype(jnp.bfloat16)
            got = jnp.dot(
                chosen,
                home[c].reshape(source_rows, width),
                preferred_element_type=jnp.float32,
            )
            if b == 0:
                packed[t] = got.astype(jnp.bfloat16)
            else:
                packed[t] = (packed[t].astype(jnp.float32) + got).astype(jnp.bfloat16)
            return carry

        lax.fori_loop(0, T, step, 0)

    def project(k):
        w_copy(k).wait()

        def step(i, carry):
            t, n = i // tiles, lax.rem(i, tiles)
            cols = pl.ds(pl.multiple_of(n * tile, tile), tile)
            part = jnp.dot(packed[t], wbuf[k, :, cols], preferred_element_type=jnp.float32)
            if k > 0:
                part = part + acc[t, :, cols]
            acc[t, :, cols] = part
            return carry

        lax.fori_loop(0, T * tiles, step, 0)

    def piece(n):
        return pl.ds(pl.multiple_of(n * tile, tile), tile)

    def rs_copy(direction, s, n):
        landing = from_left if direction == 0 else from_right
        target = rank + 1 if direction == 0 else rank - 1
        return pltpu.make_async_remote_copy(
            src_ref=own.at[s, :, piece(n)],
            dst_ref=landing.at[s, :, piece(n)],
            send_sem=rs_send.at[direction, s, n],
            recv_sem=rs_recv.at[direction, s, n],
            device_id=(me, target),
            device_id_type=MESH,
        )

    def rs_arrival(direction, s, n):
        landing = from_left if direction == 0 else from_right
        place_at = landing.at[s, :, piece(n)]
        origin = rank - 1 if direction == 0 else rank + 1
        return pltpu.make_async_remote_copy(
            src_ref=place_at,
            dst_ref=place_at,
            send_sem=rs_send.at[direction, s, n],
            recv_sem=rs_recv.at[direction, s, n],
            device_id=(me, origin),
            device_id_type=MESH,
        )

    def project_last(k):
        w_copy(k).wait()

        def step(i, carry):
            order, n = i // tiles, lax.rem(i, tiles)
            depth = order // 2
            s = jnp.where(lax.rem(order, 2) == 0, T - 1 - depth, depth)
            cols = piece(n)
            part = jnp.dot(packed[s], wbuf[k, :, cols], preferred_element_type=jnp.float32)
            if k > 0:
                part = part + acc[s, :, cols]
            own[s, :, cols] = part.astype(jnp.bfloat16)

            @pl.when((rank == 0) & (s > 0))
            def _():
                rs_copy(0, s, n).start()

            @pl.when((rank == T - 1) & (s < T - 1))
            def _():
                rs_copy(1, s, n).start()

            return carry

        lax.fori_loop(0, T * tiles, step, 0)

    def relay(i, carry):
        order, n = i // tiles, lax.rem(i, tiles)
        cols = piece(n)
        s_right, s_left = T - 1 - order, order

        @pl.when((rank > 0) & (s_right > rank))
        def _():
            rs_arrival(0, s_right, n).wait_recv()
            own[s_right, :, cols] = (
                own[s_right, :, cols].astype(jnp.float32)
                + from_left[s_right, :, cols].astype(jnp.float32)
            ).astype(jnp.bfloat16)
            rs_copy(0, s_right, n).start()

        @pl.when((rank < T - 1) & (s_left < rank))
        def _():
            rs_arrival(1, s_left, n).wait_recv()
            own[s_left, :, cols] = (
                own[s_left, :, cols].astype(jnp.float32)
                + from_right[s_left, :, cols].astype(jnp.float32)
            ).astype(jnp.bfloat16)
            rs_copy(1, s_left, n).start()

        return carry

    def settle(n, carry):
        cols = piece(n)
        acc[0, :, cols] = own[rank, :, cols].astype(jnp.float32)

        @pl.when(rank > 0)
        def _():
            rs_arrival(0, rank, n).wait_recv()
            acc[0, :, cols] = acc[0, :, cols] + from_left[rank, :, cols].astype(jnp.float32)

        @pl.when(rank < T - 1)
        def _():
            rs_arrival(1, rank, n).wait_recv()
            acc[0, :, cols] = acc[0, :, cols] + from_right[rank, :, cols].astype(jnp.float32)

        o_ref[:, cols] = acc[0, :, cols].astype(jnp.bfloat16)
        return carry

    def drain(i, carry):
        s, n = i // tiles, lax.rem(i, tiles)

        @pl.when(s > rank)
        def _():
            rs_copy(0, s, n).wait_send()

        @pl.when(s < rank)
        def _():
            rs_copy(1, s, n).wait_send()

        return carry

    for c in range(min(AHEAD, chunks)):
        start_kv(c)
    for k in range(kv_local):
        w_copy(k).start()

    def absorb(c):
        k, b = divmod(c, GROUP_REQ)
        finish_ag(c)
        pack(c)
        if b == GROUP_REQ - 1:
            if k == kv_local - 1:
                project_last(k)
            else:
                project(k)

    for c in range(chunks):
        wait_kv(c)
        if c + AHEAD < chunks:
            start_kv(c + AHEAD)
        attend(c)
        start_ag(c)
        if c > 0:
            absorb(c - 1)
    absorb(chunks - 1)
    lax.fori_loop(0, T * tiles, relay, 0)
    lax.fori_loop(0, tiles, settle, 0)
    lax.fori_loop(0, T * tiles, drain, 0)
    for c in range(chunks):
        for which in range(2):
            for o in range(1, T):
                kv_copy(c, o, which).wait_send()
        for o in range(half):
            ag_copy(c, o).wait_send()
        for o in range(1, half):
            fw_copy(c, o).wait_send()


def body(
    queries,
    draft_keys,
    draft_values,
    cache_keys,
    cache_values,
    out_weight,
    cache_lengths,
    draft_lengths,
    dest_group,
    dest_offset,
):
    T = lax.axis_size("tensor")
    D = lax.axis_size("dp")
    local_heads = HEADS // T
    group_heads = HEADS // KV_HEADS
    kv_local = max(1, local_heads // group_heads)
    width = local_heads // kv_local * HEAD_DIM
    cache = cache_keys.shape[1] * T
    out_cols = out_weight.shape[1]
    block_rows = PACK * D // T
    tiles = out_cols // min(512, out_cols)
    chunks = kv_local * GROUP_REQ
    half = D // 2
    vmem = pl.BlockSpec(memory_space=pltpu.VMEM)
    smem = pl.BlockSpec(memory_space=pltpu.SMEM)
    anywhere = pl.BlockSpec(memory_space=pl.ANY)
    dma = pltpu.SemaphoreType.DMA
    bf16 = jnp.bfloat16
    return pl.pallas_call(
        functools.partial(kernel, D, T),
        out_shape=jax.ShapeDtypeStruct((block_rows, out_cols), bf16),
        in_specs=[vmem] * 3 + [anywhere] * 3 + [smem] * 4,
        out_specs=vmem,
        scratch_shapes=[
            pltpu.VMEM((kv_local, GROUP_REQ, cache, HEAD_DIM), bf16),
            pltpu.VMEM((kv_local, GROUP_REQ, cache, HEAD_DIM), bf16),
            pltpu.VMEM((kv_local, width, out_cols), bf16),
            pltpu.VMEM((chunks, D, DRAFT, width), bf16),
            pltpu.VMEM((T, block_rows, width), bf16),
            pltpu.VMEM((T, block_rows, out_cols), jnp.float32),
            pltpu.VMEM((T, block_rows, out_cols), bf16),
            pltpu.VMEM((T, block_rows, out_cols), bf16),
            pltpu.VMEM((T, block_rows, out_cols), bf16),
            dma((chunks, 2)),
            dma((kv_local,)),
            dma((chunks, T, 2)),
            dma((chunks, T, 2)),
            dma((chunks, half)),
            dma((chunks, half)),
            dma((chunks, half)),
            dma((chunks, half)),
            dma((2, T, tiles)),
            dma((2, T, tiles)),
        ],
        compiler_params=pltpu.CompilerParams(
            collective_id=0, has_side_effects=True, vmem_limit_bytes=60 * 2**20
        ),
    )(
        queries,
        draft_keys,
        draft_values,
        cache_keys,
        cache_values,
        out_weight,
        cache_lengths,
        draft_lengths,
        dest_group,
        dest_offset,
    )


def solution(mesh):
    in_specs = (
        P("dp", "tensor"),
        P("dp", None),
        P("dp", None),
        P("dp", "tensor", None),
        P("dp", "tensor", None),
        P("tensor", "dp"),
        P("dp"),
        P(),
        P(),
        P(),
    )
    out_specs = P("tensor", "dp")
    return jax.shard_map(body, mesh=mesh, in_specs=in_specs, out_specs=out_specs, check_vma=False)
```
